1024 devices in a mesh: dp: 32 (over z), expert: 32 (over x, y, core).
Axes of the slice: x: 4, y: 4, z: 32, core: 2. Of those that a mesh axis runs over, the one named last changes fastest.
Arguments:
- tokens: bfloat16 [32, 4096, 2048], P('expert', 'dp'), may hold values from -12 to 12
- routes: int32 [32, 4096, 2], P('expert', 'dp'), may hold values from 0 to 31, all different within a row; in each aligned block of 128 rows (0 to 127, 128 to 255, ..., all dimensions but the last counted through in order) at most 10 rows name the same one
- gate_code: int32 [32, 4096, 2], P('expert', 'dp'), may hold values from 0 to 15
- gate_table: float32 [16], replicated, may hold values from 0.1 to 1
- w_gate: bfloat16 [32, 2048, 704], P('expert'), may hold values from -0.125 to 0.125
- w_up: bfloat16 [32, 2048, 704], P('expert'), may hold values from -0.125 to 0.125
- w_down: bfloat16 [32, 704, 2048], P('expert'), may hold values from -0.7 to 0.7
- norm_gain: float32 [2048], replicated, may hold values from 0.25 to 1.75
Outputs:
- relaid_out: bfloat16 [32, 4096, 2048], P('expert', None, 'dp')
The draws below stay inside these ranges and needn't reach their ends.
Inputs may be any that keep to these rules, and one draw needn't show every extreme that they name: Within the 128 tokens of one device (aligned blocks of positions) no expert is named by more than 10 routes, a bound that some block reaches; a token's two experts differ.
All inputs are finite; a program needn't handle non-finite values.
Results may differ from the reference program's by a relative error of at most 0.0064.
Values may be sent and summed in bfloat16 or wider, within the bound.
A program may use at most 32 MiB of HBM per device.

```python
import math
import jax
import jax.numpy as jnp
import numpy as np
from jax import lax

D = 2048
FF = 704
LEVELS = 16
TOK_DEV = 128
EXPERTS = 32
CAP = 10
LENGTH = 4096
SEQS = 32
N_DP = 32


def draw_tokens(key, part):
    key_main, key_rows = jax.random.split(key, 2)
    row_scale = 10.0 ** jax.random.uniform(key_rows, (SEQS, LENGTH, 1), jnp.float32, -0.5, 0.5)
    noise_main = jax.random.normal(key_main, (SEQS, LENGTH, D), jnp.float32)
    return jnp.clip(noise_main * row_scale, -12.0, 12.0).astype(jnp.bfloat16)


def draw_w_down(key, part):
    column_scale = 10.0 ** (jnp.arange(D, dtype=jnp.float32) / D - 0.5)
    noise_main = jax.random.normal(key, (EXPERTS, FF, D), jnp.float32)
    values = noise_main * FF ** (-0.5) * column_scale[None, None, :]
    return jnp.clip(values, -0.7, 0.7).astype(jnp.bfloat16)


def touch_ends(values, key, low, top_value):
    longest = values.shape.index(max(values.shape))
    spots = []
    for shift in (0, 1):
        where = [jax.random.randint(jax.random.fold_in(key, axis), (), 0, length) for axis, length in enumerate(values.shape)]
        where[longest] = (where[longest] + shift) % values.shape[longest]
        spots.append(tuple(where))
    return values.at[spots[0]].set(low).at[spots[1]].set(top_value)


def level_of(stream_key, shape, pieces, least, largest):
    factor_of, own = 1.0, jax.random.fold_in(stream_key, 6)
    for axis_at, parts in pieces:
        heights = jnp.exp(jax.random.uniform(jax.random.fold_in(own, axis_at), (parts,), jnp.float32, least / len(pieces), largest / len(pieces)))
        factor_of = factor_of * jnp.repeat(heights, shape[axis_at] // parts).reshape([-1 if axis == axis_at else 1 for axis in range(len(shape))])
    return factor_of


def deal_out(stream_key, own, number, rows, amount, top, bound, lean):
    order = jax.random.permutation(stream_key, amount)
    crowded, usual = shares(amount, rows * top, bound, lean, True), shares(amount, rows * top, bound, lean, False)
    places = jnp.arange(amount)

    def named(lengths, offset_by):
        used = int((lengths > 0).sum())
        fixed = max(1, used // 4)
        moved = fixed + (places - fixed + offset_by * (used - fixed)) % max(1, amount - fixed)
        return jnp.zeros((amount,), jnp.int32).at[order[jnp.where(places < fixed, places, moved)]].set(jnp.asarray(lengths, jnp.int32))

    lengths = jnp.where(number % 4 == 0, named(crowded, number // 4), named(usual, number - number // 4 - 1))
    mixed = jax.random.permutation(jax.random.fold_in(own, 3), amount)
    giver, receiver = mixed[0:amount // 2 * 2:2], mixed[1:amount // 2 * 2:2]
    room = jnp.minimum(lengths[giver] - 1, bound - lengths[receiver]) // 2
    room = jnp.where((giver == order[0]) | (receiver == order[0]) | (lengths[receiver] == 0), 0, jnp.maximum(room, 0))
    moved = jax.random.randint(jax.random.fold_in(own, 4), (amount // 2,), 0, 1 << 20) % (room + 1)
    lengths = lengths.at[giver].add(-moved).at[receiver].add(moved)
    labels = jnp.searchsorted(jnp.cumsum(lengths), jnp.arange(rows * top), side="right").astype(jnp.int32)
    table = labels.reshape(top, rows).T
    table = table[jax.random.permutation(jax.random.fold_in(own, 1), rows)]
    offset_by = jax.random.randint(jax.random.fold_in(own, 2), (rows, 1), 0, top)
    return jnp.take_along_axis(table, (jnp.arange(top)[None, :] + offset_by) % top, axis=1)


def shares(amount, total, bound, skew, full):
    loads = [(1 << 20) // math.isqrt(standing ** skew) + 1 for standing in range(1, amount + 1)]
    largest = bound if full else min(bound, max(-(-total // amount), total * loads[0] // sum(loads)))
    least = 1 if total - largest >= amount - 1 else 0
    given, rest = [largest] + [least] * (amount - 1), total - largest - least * (amount - 1)
    while rest > 0:
        candidates = [i for i in range(1, amount) if given[i] < largest] or [i for i in range(1, amount) if given[i] < bound]
        pool, budget = sum([loads[i] for i in candidates]), rest
        for i in candidates:
            extra = min(bound - given[i], max(1, budget * loads[i] // pool), rest)
            given[i] = given[i] + extra
            rest = rest - extra
    return np.array(given)


def scatter_about(own_key, dims, spread, limit, cuts=(), held_as=jnp.bfloat16):
    factor_of = level_of(own_key, dims, cuts, -0.22, 0.18) if cuts else 1.0
    entries = jax.random.normal(own_key, dims, jnp.float32) * spread * factor_of
    return jnp.minimum(jnp.maximum(entries, -limit), limit).astype(held_as)


def setup_inputs(seed: int = 0) -> dict:
    keys = jax.random.split(jax.random.key(seed), 9)
    tokens = draw_tokens(jax.random.fold_in(keys[8], 71), 0)
    routes_keys = jax.random.split(jax.random.fold_in(keys[1], 1), SEQS * LENGTH // TOK_DEV)
    routes_turns = jax.random.permutation(jax.random.fold_in(keys[1], 3), SEQS * LENGTH // TOK_DEV)
    routes = jax.vmap(lambda own, number: deal_out(jax.random.fold_in(keys[1], 2), own, number, TOK_DEV, EXPERTS, 2, CAP, 2))(routes_keys, routes_turns).reshape((SEQS, LENGTH, 2))
    gate_code = touch_ends(jax.random.randint(keys[2], (SEQS, LENGTH, 2), 0, LEVELS), jax.random.fold_in(keys[2], 1), 0, LEVELS - 1).astype(jnp.int32)
    gate_table = jnp.clip(jnp.exp(jax.random.uniform(keys[3], (LEVELS,), jnp.float32, math.log(0.1), math.log(1.0))), 0.1, 1.0)
    w_gate = scatter_about(keys[4], (EXPERTS, D, FF), D ** -0.5, 0.125, ((0, 32),))
    w_up = scatter_about(keys[5], (EXPERTS, D, FF), D ** -0.5, 0.125, ((0, 32),))
    w_down = draw_w_down(jax.random.fold_in(keys[8], 71), 0)
    norm_gain = jnp.clip(1.0 + 0.15 * jax.random.normal(keys[7], (D,), jnp.float32), 0.25, 1.75)
    return dict(tokens=tokens, routes=routes, gate_code=gate_code, gate_table=gate_table, w_gate=w_gate, w_up=w_up, w_down=w_down, norm_gain=norm_gain)


epsilon = 1e-06

def reference(tokens, routes, gate_code, gate_table, w_gate, w_up, w_down, norm_gain):
    blocks = SEQS * N_DP
    flat_tok = tokens.reshape(-1, D)
    block_routes = routes.reshape(blocks, 2 * TOK_DEV)
    onehot = (block_routes[:, :, None] == jnp.arange(EXPERTS, dtype=jnp.int32)[None, None, :]).astype(jnp.int32)
    slot_pos = lax.optimization_barrier(jnp.sum((jnp.cumsum(onehot, axis=1) - onehot) * onehot, axis=2))
    block_base = (jnp.arange(blocks, dtype=jnp.int32) * CAP)[:, None]
    position = (block_base + slot_pos).reshape(-1, 2).astype(jnp.int32)
    expert_ids = routes.reshape(-1, 2)
    levels = gate_table.shape[0]
    level_match = gate_code.reshape(-1, 2)[:, :, None] == jnp.arange(levels, dtype=jnp.int32)[None, None, :]
    weights = lax.optimization_barrier(jnp.sum(jnp.where(level_match, gate_table[None, None, :], 0.0), axis=2))
    rows_total = blocks * CAP

    def one_expert(summed, inputs):
        expert_index, gate_w, up_w, down_w = inputs
        buffer = jnp.zeros((rows_total, D), jnp.bfloat16)
        for column in range(2):
            chosen = expert_ids[:, column] == expert_index
            target = jnp.where(chosen, position[:, column], rows_total)
            buffer = buffer.at[target].set(flat_tok, mode='drop')
        wide_buffer = buffer.astype(jnp.float32)
        gate_act = jnp.dot(wide_buffer, gate_w.astype(jnp.float32))
        up_act = jnp.dot(wide_buffer, up_w.astype(jnp.float32))
        hidden = (jax.nn.silu(gate_act) * up_act).astype(jnp.bfloat16)
        result = jnp.dot(hidden.astype(jnp.float32), down_w.astype(jnp.float32)).astype(jnp.bfloat16)
        for column in range(2):
            chosen = expert_ids[:, column] == expert_index
            picked = result[jnp.minimum(position[:, column], rows_total - 1)].astype(jnp.float32)
            summed = summed + jnp.where(chosen[:, None], weights[:, column:column + 1] * picked, 0.0)
        return (summed, None)
    start = jnp.zeros((flat_tok.shape[0], D), jnp.float32)
    summed, _ = lax.scan(one_expert, start, (jnp.arange(EXPERTS, dtype=jnp.int32), w_gate, w_up, w_down))
    rounded = lax.optimization_barrier(summed.astype(jnp.bfloat16))
    widened = rounded.astype(jnp.float32)
    inv_rms = lax.rsqrt(lax.optimization_barrier(jnp.mean(widened * widened, axis=1, keepdims=True)) + epsilon)
    return (widened * inv_rms * norm_gain[None, :]).astype(jnp.bfloat16).reshape(SEQS, LENGTH, D)
```

```python
import functools

import jax
import jax.numpy as jnp
from jax import lax
from jax.experimental import pallas as pl
from jax.experimental.pallas import tpu as pltpu
from jax.sharding import PartitionSpec as P

epsilon = 1e-06
MESH = pl.DeviceIdType.MESH
BF16 = jnp.bfloat16
F32 = jnp.float32

N = 32
TOK = 128
D = 2048
FF = 704
MAIN = 8
REST = 2
QUAD = 256
CHUNKS = 5


def drain(ref, count, sem):
    pltpu.make_async_copy(ref.at[pl.ds(0, count)], ref.at[pl.ds(0, count)], sem).wait()


def iota(shape, dim):
    return lax.broadcasted_iota(jnp.int32, shape, dim)


def onehot(cond):
    return jnp.where(cond, 1.0, 0.0).astype(BF16)


def slots_of(routes):
    own = [jnp.where(iota((N, TOK), 0) == routes[k : k + 1], 1.0, 0.0) for k in range(2)]
    before = jnp.where(iota((TOK, TOK), 0) < iota((TOK, TOK), 1), 1.0, 0.0).astype(BF16)
    earlier = [jnp.dot(o.astype(BF16), before, preferred_element_type=F32) for o in own]
    first = jnp.sum(own[0], axis=1, keepdims=True)
    rank0 = jnp.sum(own[0] * earlier[0], axis=0, keepdims=True)
    rank1 = jnp.sum(own[1] * (earlier[1] + first), axis=0, keepdims=True)
    return [rank0.astype(jnp.int32), rank1.astype(jnp.int32)]


def kernel(
    tok_hbm, routes_hbm, codes_hbm, table_ref, wg_hbm, wu_hbm, wd_hbm, gain_hbm, out_ref,
    tok, routes, codes, gain, wg, wu, wd,
    send, recv, rest_x, gate, up, hid, mix, ret_s, ret_r, z_s, z_r, inv_s, inv_r, ssq,
    load_sem, send_sem, recv_sem, rsend_sem, rrecv_sem, zsend_sem, zrecv_sem, isend_sem, irecv_sem,
):
    z = lax.axis_index("dp")
    e = lax.axis_index("expert")

    bar = pltpu.get_barrier_semaphore()

    @pl.loop(1, N)
    def _(d):
        pl.semaphore_signal(bar, 1, device_id={"expert": e ^ d}, device_id_type=MESH)

    @pl.loop(1, N)
    def _(d):
        pl.semaphore_signal(bar, 1, device_id={"dp": (z + d) % N}, device_id_type=MESH)

    loads = [
        pltpu.make_async_copy(a, b, load_sem.at[i])
        for i, (a, b) in enumerate(
            [(tok_hbm, tok), (routes_hbm, routes), (codes_hbm, codes), (gain_hbm, gain), (wg_hbm, wg), (wu_hbm, wu), (wd_hbm, wd)]
        )
    ]
    for load in loads:
        load.start()
    for load in loads[:3]:
        load.wait()

    to = [routes[k : k + 1, :] for k in range(2)]
    rank = slots_of(routes[...])
    main_at = [jnp.where(r < MAIN, t * MAIN + r, -1) for t, r in zip(to, rank)]
    rest_at = [jnp.where(r >= MAIN, t * REST + r - MAIN, -1) for t, r in zip(to, rank)]
    back_at = [t * 16 + r for t, r in zip(to, rank)]

    rows = iota((N * MAIN, TOK), 0)
    pick = onehot((rows == main_at[0]) | (rows == main_at[1]))
    for c in range(4):
        both = jnp.dot(pick, tok[:, c * 512 : (c + 1) * 512], preferred_element_type=F32)
        folded = jnp.stack([both[:, :256].reshape(N, 8, 256), both[:, 256:].reshape(N, 8, 256)], axis=1)
        send[c * N : (c + 1) * N] = folded.reshape(N, 16, 256).astype(BF16)
    rows = iota((N * 16, TOK), 0)
    held = (rows // 8 == rest_at[0]) | (rows // 8 == rest_at[1])
    total = jnp.zeros((N * 16, 256), F32)
    for q in range(8):
        part = onehot(held & (rows % 8 == q))
        total += jnp.dot(part, tok[:, q * 256 : (q + 1) * 256], preferred_element_type=F32)
    send[4 * N : 5 * N] = total.reshape(N, 16, 256).astype(BF16)

    pl.semaphore_wait(bar, 2 * (N - 1))

    for c in (4, 0, 1, 2, 3):

        @pl.loop(1, N)
        def _(d):
            t = e ^ d
            pltpu.make_async_remote_copy(
                send.at[c * N + t], recv.at[c * N + e], send_sem, recv_sem.at[c], device_id={"expert": t}, device_id_type=MESH
            ).start()

        recv[c * N + e] = send[c * N + e]

    weight = [jnp.zeros((1, TOK), F32) for _ in range(2)]
    for k in range(2):
        for level in range(16):
            weight[k] = jnp.where(codes[k : k + 1, :] == level, table_ref[level], weight[k])
    rows = iota((N * 16, TOK), 0)
    wide = jnp.where(rows == back_at[0], weight[0], 0.0) + jnp.where(rows == back_at[1], weight[1], 0.0)
    wide = wide.T
    high = wide.astype(BF16)
    mix[:TOK] = high
    mix[TOK:] = (wide - high.astype(F32)).astype(BF16)
    ssq[...] = jnp.zeros_like(ssq)

    for load in loads[4:6]:
        load.wait()
    drain(recv, N - 1, recv_sem.at[4])
    at = iota((N * 16, N * 16), 0)
    unfold = onehot(iota((N * 16, N * 16), 1) == (at % 64) * 8 + at // 64)
    rest_x[...] = jnp.dot(unfold, recv[4 * N : 5 * N].reshape(N * 16, 256), preferred_element_type=F32).astype(BF16)
    for c in range(4):
        drain(recv, N - 1, recv_sem.at[c])
        halves = [
            jnp.concatenate(
                [recv[c * N : (c + 1) * N, h * 8 : (h + 1) * 8].reshape(N * 8, 256), rest_x[(2 * c + h) * 64 : (2 * c + h + 1) * 64]],
                axis=0,
            )
            for h in range(2)
        ]
        x = jnp.concatenate(halves, axis=1)
        for w, acc in ((wg, gate), (wu, up)):
            part = lax.dot_general(x, w[:, c * 512 : (c + 1) * 512], (((1,), (1,)), ((), ())), preferred_element_type=F32)
            if c == 0:
                acc[...] = part
            else:
                acc[...] += part
    g = gate[...]
    h = (g / (1.0 + jnp.exp(-g)) * up[...]).astype(BF16)
    hid[: N * 8] = h[: N * 8]
    spread = onehot(iota((N * 8, 64), 1) == (iota((N * 8, 64), 0) // 8) * 2 + iota((N * 8, 64), 0) % 8)
    spread = jnp.where(iota((N * 8, 64), 0) % 8 < 2, spread, jnp.zeros((), BF16))
    hid[N * 8 :] = jnp.dot(spread, h[N * 8 :], preferred_element_type=F32).astype(BF16)
    loads[6].wait()
    loads[3].wait()

    def quad_of(k):
        far = (k + 1) // 2
        return (z // 4 + 4 + jnp.where(k % 2 == 1, -far, far)) % 8

    def expert_part(k):
        quad = quad_of(k)
        cols = pl.ds(pl.multiple_of(quad * QUAD, QUAD), QUAD)
        out = jnp.dot(hid[...], wd[:, cols], preferred_element_type=F32)
        both = jnp.stack([out[: N * 8].reshape(N, 8, QUAD), out[N * 8 :].reshape(N, 8, QUAD)], axis=1)
        ret_s[pl.ds(k * N, N)] = both.reshape(N, 16, QUAD).astype(BF16)

        @pl.loop(1, N)
        def _(d):
            t = e ^ d
            pltpu.make_async_remote_copy(
                ret_s.at[k * N + t], ret_r.at[k * N + e], rsend_sem, rrecv_sem.at[k], device_id={"expert": t}, device_id_type=MESH
            ).start()

        ret_r[k * N + e] = ret_s[k * N + e]

    def home_part(k):
        quad = quad_of(k)
        drain(ret_r, N - 1, rrecv_sem.at[k])
        block = ret_r[pl.ds(k * N, N)].reshape(N * 16, QUAD)
        pair = jnp.dot(mix[...], block, preferred_element_type=F32)
        comb = (pair[:TOK] + pair[TOK:]).astype(BF16).astype(F32).T
        ssq[...] += jnp.sum(comb * comb, axis=0, keepdims=True)
        base = pl.multiple_of(quad * QUAD, QUAD)
        z_s[pl.ds(base, QUAD)] = comb.astype(BF16)

        @pl.loop(0, 4)
        def _(b):
            t = quad * 4 + b

            @pl.when(t != z)
            def _():
                pltpu.make_async_remote_copy(
                    z_s.at[pl.ds(pl.multiple_of(t * 64, 64), 64)], z_r.at[z], zsend_sem, zrecv_sem, device_id={"dp": t}, device_id_type=MESH
                ).start()

    expert_part(0)

    @pl.loop(1, 8)
    def _(k):
        expert_part(k)
        home_part(k - 1)

    home_part(7)

    inv_s[...] = lax.rsqrt(ssq[...] * (1.0 / D) + epsilon)

    @pl.loop(1, N)
    def _(d):
        pltpu.make_async_remote_copy(
            inv_s, inv_r.at[z], isend_sem, irecv_sem, device_id={"dp": (z + d) % N}, device_id_type=MESH
        ).start()

    inv_r[z] = inv_s[...]
    z_r[z] = z_s[pl.ds(pl.multiple_of(z * 64, 64), 64)]

    line = jnp.broadcast_to(gain[pl.ds(z // 2, 1), :], (64, 128))
    mine = iota((64, 128), 1) == iota((64, 128), 0) + 64 * (z % 2)
    column = jnp.sum(jnp.where(mine, line, 0.0), axis=1, keepdims=True)

    drain(send, CHUNKS * (N - 1), send_sem)
    drain(ret_s, 8 * (N - 1), rsend_sem)
    drain(z_s, (N - 1) * 64, zsend_sem)
    drain(inv_r, N - 1, isend_sem)
    drain(z_r, N - 1, zrecv_sem)
    drain(inv_r, N - 1, irecv_sem)
    for s in range(N):
        out_ref[:, s * TOK : (s + 1) * TOK] = (z_r[s].astype(F32) * inv_r[s] * column).astype(BF16)


def local(tokens, routes, gate_code, gate_table, w_gate, w_up, w_down, norm_gain):
    anywhere = pl.BlockSpec(memory_space=pl.ANY)
    dma = pltpu.SemaphoreType.DMA
    relaid = pl.pallas_call(
        kernel,
        out_shape=jax.ShapeDtypeStruct((D // N, N * TOK), BF16),
        in_specs=[anywhere] * 3 + [pl.BlockSpec(memory_space=pltpu.SMEM)] + [anywhere] * 4,
        out_specs=pl.BlockSpec(memory_space=pltpu.VMEM),
        scratch_shapes=[
            pltpu.VMEM((TOK, D), BF16),
            pltpu.VMEM((2, TOK), jnp.int32),
            pltpu.VMEM((2, TOK), jnp.int32),
            pltpu.VMEM((16, 128), F32),
            pltpu.VMEM((FF, D), BF16),
            pltpu.VMEM((FF, D), BF16),
            pltpu.VMEM((FF, D), BF16),
            pltpu.VMEM((CHUNKS * N, 16, 256), BF16),
            pltpu.VMEM((CHUNKS * N, 16, 256), BF16),
            pltpu.VMEM((N * 16, 256), BF16),
            pltpu.VMEM((320, FF), F32),
            pltpu.VMEM((320, FF), F32),
            pltpu.VMEM((N * 16, FF), BF16),
            pltpu.VMEM((2 * TOK, N * 16), BF16),
            pltpu.VMEM((8 * N, 16, QUAD), BF16),
            pltpu.VMEM((8 * N, 16, QUAD), BF16),
            pltpu.VMEM((D, TOK), BF16),
            pltpu.VMEM((N, 64, TOK), BF16),
            pltpu.VMEM((1, TOK), F32),
            pltpu.VMEM((N, 1, TOK), F32),
            pltpu.VMEM((1, TOK), F32),
            dma((7,)), dma, dma((CHUNKS,)), dma, dma((8,)), dma, dma, dma, dma,
        ],
        compiler_params=pltpu.CompilerParams(collective_id=0, has_side_effects=True, vmem_limit_bytes=48 << 20),
        cost_estimate=pl.CostEstimate(flops=3 << 30, bytes_accessed=10 << 20, transcendentals=320 * FF),
    )(
        tokens[0],
        routes[0].T,
        gate_code[0].T,
        gate_table,
        jnp.swapaxes(w_gate[0], 0, 1),
        jnp.swapaxes(w_up[0], 0, 1),
        w_down[0],
        norm_gain.reshape(16, 128),
    )
    return relaid.T[None]


def solution(mesh):
    in_specs = (
        P("expert", "dp", None),
        P("expert", "dp", None),
        P("expert", "dp", None),
        P(),
        P("expert", None, None),
        P("expert", None, None),
        P("expert", None, None),
        P(),
    )
    out_specs = P("expert", None, "dp")
    return jax.shard_map(local, mesh=mesh, in_specs=in_specs, out_specs=out_specs, check_vma=False)
```

```python
import functools

import jax
import jax.numpy as jnp
from jax import lax
from jax.experimental import pallas as pl
from jax.experimental.pallas import tpu as pltpu
from jax.sharding import PartitionSpec as P

epsilon = 1e-06
MESH = pl.DeviceIdType.MESH
BF16 = jnp.bfloat16
F32 = jnp.float32

N = 32
TOK = 128
D = 2048
FF = 704
MAIN = 8
REST = 2
QUAD = 256
RELAY = 31
LAG = 2
CHUNKS = 5


def drain(ref, count, sem):
    pltpu.make_async_copy(ref.at[pl.ds(0, count)], ref.at[pl.ds(0, count)], sem).wait()


def iota(shape, dim):
    return lax.broadcasted_iota(jnp.int32, shape, dim)


def onehot(cond):
    return jnp.where(cond, 1.0, 0.0).astype(BF16)


def slots_of(routes):
    own = [jnp.where(iota((N, TOK), 0) == routes[k : k + 1], 1.0, 0.0) for k in range(2)]
    before = jnp.where(iota((TOK, TOK), 0) < iota((TOK, TOK), 1), 1.0, 0.0).astype(BF16)
    earlier = [jnp.dot(o.astype(BF16), before, preferred_element_type=F32) for o in own]
    first = jnp.sum(own[0], axis=1, keepdims=True)
    rank0 = jnp.sum(own[0] * earlier[0], axis=0, keepdims=True)
    rank1 = jnp.sum(own[1] * (earlier[1] + first), axis=0, keepdims=True)
    return [rank0.astype(jnp.int32), rank1.astype(jnp.int32)]


def kernel(
    tok_hbm, routes_hbm, codes_hbm, table_ref, wg_hbm, wu_hbm, wd_hbm, gain_hbm, out_ref,
    tok, routes, codes, gain, wg, wu, wd,
    send, recv, rest_x, gate, up, hid, mix, fold, unfold, ret_s, ret_r, back_x, z_s, z_r, inv_s, inv_r, ssq,
    load_sem, send_sem, recv_sem, rsend_sem, rrecv_sem, zsend_sem, zrecv_sem, isend_sem, irecv_sem, plane_sem, open_sem,
):
    z = lax.axis_index("dp")
    e = lax.axis_index("expert")

    bar = pltpu.get_barrier_semaphore()

    @pl.loop(1, N)
    def _(d):
        @pl.when(e ^ d != RELAY)
        def _():
            pl.semaphore_signal(bar, 1, device_id={"expert": e ^ d}, device_id_type=MESH)

    loads = [
        pltpu.make_async_copy(a, b, load_sem.at[i])
        for i, (a, b) in enumerate(
            [(tok_hbm, tok), (routes_hbm, routes), (codes_hbm, codes), (gain_hbm, gain), (wg_hbm, wg), (wu_hbm, wu), (wd_hbm, wd)]
        )
    ]
    for load in loads:
        load.start()
    for load in loads[:3]:
        load.wait()

    to = [routes[k : k + 1, :] for k in range(2)]
    rank = slots_of(routes[...])
    main_at = [jnp.where(r < MAIN, t * MAIN + r, -1) for t, r in zip(to, rank)]
    rest_at = [jnp.where(r >= MAIN, t * REST + r - MAIN, -1) for t, r in zip(to, rank)]

    rows = iota((N * MAIN, TOK), 0)
    pick = onehot((rows == main_at[0]) | (rows == main_at[1]))
    for c in range(4):
        both = jnp.dot(pick, tok[:, c * 512 : (c + 1) * 512], preferred_element_type=F32)
        folded = jnp.stack([both[:, :256].reshape(N, 8, 256), both[:, 256:].reshape(N, 8, 256)], axis=1)
        send[c * N : (c + 1) * N] = folded.reshape(N, 16, 256).astype(BF16)
    rows = iota((N * 16, TOK), 0)
    held = (rows // 8 == rest_at[0]) | (rows // 8 == rest_at[1])
    total = jnp.zeros((N * 16, 256), F32)
    for q in range(8):
        part = onehot(held & (rows % 8 == q))
        total += jnp.dot(part, tok[:, q * 256 : (q + 1) * 256], preferred_element_type=F32)
    send[4 * N : 5 * N] = total.reshape(N, 16, 256).astype(BF16)

    at = iota((N * 16, N * 16), 0)
    unfold[...] = onehot(iota((N * 16, N * 16), 1) == (at % 64) * 8 + at // 64)
    fold[...] = onehot(iota((N * 16, N * 16), 1) == (at % 8) * 64 + at // 8)

    @pl.when(e != RELAY)
    def _():
        pl.semaphore_wait(bar, N - 1)

    @pl.when(e == RELAY - 1)
    def _():
        pl.semaphore_signal(plane_sem, 1, device_id={"expert": RELAY}, device_id_type=MESH)

    @pl.when(e == RELAY)
    def _():
        pl.semaphore_wait(plane_sem, 1)

        @pl.loop(1, N)
        def _(d):
            pl.semaphore_signal(bar, 1, device_id={"dp": (z + d) % N}, device_id_type=MESH)

    for c in (4, 0, 1, 2, 3):

        @pl.loop(1, N)
        def _(d):
            t = e ^ d
            pltpu.make_async_remote_copy(
                send.at[c * N + t], recv.at[c * N + e], send_sem, recv_sem.at[c], device_id={"expert": t}, device_id_type=MESH
            ).start()

        recv[c * N + e] = send[c * N + e]

    weight = [jnp.zeros((1, TOK), F32) for _ in range(2)]
    for k in range(2):
        for level in range(16):
            weight[k] = jnp.where(codes[k : k + 1, :] == level, table_ref[level], weight[k])
    rows = iota((384, TOK), 0)
    wide = jnp.zeros((384, TOK), F32)
    for k in range(2):
        wide += jnp.where(rows == jnp.where(rank[k] < MAIN, main_at[k], N * MAIN + rest_at[k]), weight[k], 0.0)
    wide = wide.T[:, :320]
    high = wide.astype(BF16)
    mix[:TOK] = high
    mix[TOK:] = (wide - high.astype(F32)).astype(BF16)
    ssq[...] = jnp.zeros_like(ssq)

    for load in loads[4:6]:
        load.wait()
    drain(recv, N - 1, recv_sem.at[4])
    rest_x[...] = jnp.dot(unfold[...], recv[4 * N : 5 * N].reshape(N * 16, 256), preferred_element_type=F32).astype(BF16)
    for c in range(4):
        drain(recv, N - 1, recv_sem.at[c])
        halves = [
            jnp.concatenate(
                [recv[c * N : (c + 1) * N, h * 8 : (h + 1) * 8].reshape(N * 8, 256), rest_x[(2 * c + h) * 64 : (2 * c + h + 1) * 64]],
                axis=0,
            )
            for h in range(2)
        ]
        x = jnp.concatenate(halves, axis=1)
        for w, acc in ((wg, gate), (wu, up)):
            part = lax.dot_general(x, w[:, c * 512 : (c + 1) * 512], (((1,), (1,)), ((), ())), preferred_element_type=F32)
            if c == 0:
                acc[...] = part
            else:
                acc[...] += part
    g = gate[...]
    hid[...] = (g / (1.0 + jnp.exp(-g)) * up[...]).astype(BF16)
    loads[6].wait()
    loads[3].wait()

    def quad_of(k):
        far = (k + 1) // 2
        return (z // 4 + 4 + jnp.where(k % 2 == 1, -far, far)) % 8

    def columns(quad):
        return wd[:, pl.ds(pl.multiple_of(quad * QUAD, QUAD), QUAD)]

    def give_back(at, block):
        ret_s[pl.ds(at * N, N)] = block.reshape(N, 16, 128).astype(BF16)

        @pl.loop(1, N)
        def _(d):
            t = e ^ d
            pltpu.make_async_remote_copy(
                ret_s.at[at * N + t], ret_r.at[at * N + e], rsend_sem, rrecv_sem.at[at], device_id={"expert": t}, device_id_type=MESH
            ).start()

        ret_r[at * N + e] = ret_s[at * N + e]

    def expert_rest(half):
        pieces = []
        for i in range(4):
            out = jnp.dot(hid[N * MAIN :], columns(quad_of(half * 4 + i)), preferred_element_type=F32).astype(BF16)
            pieces += [out[:, :128], out[:, 128:]]
        give_back(8 + half, jnp.dot(fold[...], jnp.concatenate(pieces, axis=0), preferred_element_type=F32))

    def expert_main(k):
        out = jnp.dot(hid[: N * MAIN], columns(quad_of(k)), preferred_element_type=F32)
        give_back(k, jnp.stack([out[:, :128].reshape(N, 8, 128), out[:, 128:].reshape(N, 8, 128)], axis=1))

    def home_rest(half):
        drain(ret_r, N - 1, rrecv_sem.at[8 + half])
        block = ret_r[pl.ds((8 + half) * N, N)].reshape(N * 16, 128)
        back_x[...] = jnp.dot(unfold[...], block, preferred_element_type=F32).reshape(8, 64, 128).astype(BF16)

    def home_main(k):
        quad = quad_of(k)
        drain(ret_r, N - 1, rrecv_sem.at[k])
        halves = [
            jnp.concatenate([ret_r[pl.ds(k * N, N), h * 8 : (h + 1) * 8].reshape(N * 8, 128), back_x[2 * (k % 4) + h]], axis=0)
            for h in range(2)
        ]
        block = jnp.concatenate(halves, axis=1)
        pair = jnp.dot(mix[...], block, preferred_element_type=F32)
        comb = (pair[:TOK] + pair[TOK:]).astype(BF16).astype(F32).T
        ssq[...] += jnp.sum(comb * comb, axis=0, keepdims=True)
        base = pl.multiple_of(quad * QUAD, QUAD)
        z_s[pl.ds(base, QUAD)] = comb.astype(BF16)

        @pl.loop(0, 4)
        def _(b):
            t = quad * 4 + b

            @pl.when(t != z)
            def _():
                pltpu.make_async_remote_copy(
                    z_s.at[pl.ds(pl.multiple_of(t * 64, 64), 64)], z_r.at[z], zsend_sem, zrecv_sem, device_id={"dp": t}, device_id_type=MESH
                ).start()

    @pl.loop(0, 8 + LAG)
    def _(k):
        @pl.when((k == 0) | (k == 4))
        def _():
            expert_rest(k // 4)

        @pl.when(k < 8)
        def _():
            expert_main(k)

        @pl.when((k == LAG) & (e == RELAY))
        def _():
            pl.semaphore_wait(bar, N - 1)

            @pl.loop(1, N)
            def _(d):
                pl.semaphore_signal(open_sem, 1, device_id={"expert": e ^ d}, device_id_type=MESH)

        @pl.when((k == LAG) & (e != RELAY))
        def _():
            pl.semaphore_wait(open_sem, 1)

        @pl.when((k == LAG) | (k == LAG + 4))
        def _():
            home_rest((k - LAG) // 4)

        @pl.when(k >= LAG)
        def _():
            home_main(k - LAG)

    inv_s[...] = lax.rsqrt(ssq[...] * (1.0 / D) + epsilon)

    @pl.loop(1, N)
    def _(d):
        pltpu.make_async_remote_copy(
            inv_s, inv_r.at[z], isend_sem, irecv_sem, device_id={"dp": (z + d) % N}, device_id_type=MESH
        ).start()

    inv_r[z] = inv_s[...]
    z_r[z] = z_s[pl.ds(pl.multiple_of(z * 64, 64), 64)]

    line = jnp.broadcast_to(gain[pl.ds(z // 2, 1), :], (64, 128))
    mine = iota((64, 128), 1) == iota((64, 128), 0) + 64 * (z % 2)
    column = jnp.sum(jnp.where(mine, line, 0.0), axis=1, keepdims=True)

    drain(send, CHUNKS * (N - 1), send_sem)
    drain(ret_s, 10 * (N - 1), rsend_sem)
    drain(z_s, (N - 1) * 64, zsend_sem)
    drain(inv_r, N - 1, isend_sem)
    drain(z_r, N - 1, zrecv_sem)
    drain(inv_r, N - 1, irecv_sem)
    for s in range(N):
        out_ref[:, s * TOK : (s + 1) * TOK] = (z_r[s].astype(F32) * inv_r[s] * column).astype(BF16)


def local(tokens, routes, gate_code, gate_table, w_gate, w_up, w_down, norm_gain):
    anywhere = pl.BlockSpec(memory_space=pl.ANY)
    dma = pltpu.SemaphoreType.DMA
    relaid = pl.pallas_call(
        kernel,
        out_shape=jax.ShapeDtypeStruct((D // N, N * TOK), BF16),
        in_specs=[anywhere] * 3 + [pl.BlockSpec(memory_space=pltpu.SMEM)] + [anywhere] * 4,
        out_specs=pl.BlockSpec(memory_space=pltpu.VMEM),
        scratch_shapes=[
            pltpu.VMEM((TOK, D), BF16),
            pltpu.VMEM((2, TOK), jnp.int32),
            pltpu.VMEM((2, TOK), jnp.int32),
            pltpu.VMEM((16, 128), F32),
            pltpu.VMEM((FF, D), BF16),
            pltpu.VMEM((FF, D), BF16),
            pltpu.VMEM((FF, D), BF16),
            pltpu.VMEM((CHUNKS * N, 16, 256), BF16),
            pltpu.VMEM((CHUNKS * N, 16, 256), BF16),
            pltpu.VMEM((N * 16, 256), BF16),
            pltpu.VMEM((320, FF), F32),
            pltpu.VMEM((320, FF), F32),
            pltpu.VMEM((320, FF), BF16),
            pltpu.VMEM((2 * TOK, 320), BF16),
            pltpu.VMEM((N * 16, N * 16), BF16),
            pltpu.VMEM((N * 16, N * 16), BF16),
            pltpu.VMEM((10 * N, 16, 128), BF16),
            pltpu.VMEM((10 * N, 16, 128), BF16),
            pltpu.VMEM((8, 64, 128), BF16),
            pltpu.VMEM((D, TOK), BF16),
            pltpu.VMEM((N, 64, TOK), BF16),
            pltpu.VMEM((1, TOK), F32),
            pltpu.VMEM((N, 1, TOK), F32),
            pltpu.VMEM((1, TOK), F32),
            dma((7,)), dma, dma((CHUNKS,)), dma, dma((10,)), dma, dma, dma, dma,
            pltpu.SemaphoreType.REGULAR, pltpu.SemaphoreType.REGULAR,
        ],
        compiler_params=pltpu.CompilerParams(collective_id=0, has_side_effects=True, vmem_limit_bytes=63 << 20),
        cost_estimate=pl.CostEstimate(flops=3 << 30, bytes_accessed=10 << 20, transcendentals=320 * FF),
    )(
        tokens[0],
        routes[0].T,
        gate_code[0].T,
        gate_table,
        jnp.swapaxes(w_gate[0], 0, 1),
        jnp.swapaxes(w_up[0], 0, 1),
        w_down[0],
        norm_gain.reshape(16, 128),
    )
    return relaid.T[None]


def solution(mesh):
    in_specs = (
        P("expert", "dp", None),
        P("expert", "dp", None),
        P("expert", "dp", None),
        P(),
        P("expert", None, None),
        P("expert", None, None),
        P("expert", None, None),
        P(),
    )
    out_specs = P("expert", None, "dp")
    return jax.shard_map(local, mesh=mesh, in_specs=in_specs, out_specs=out_specs, check_vma=False)
```

```python
import functools

import jax
import jax.numpy as jnp
from jax import lax
from jax.experimental import pallas as pl
from jax.experimental.pallas import tpu as pltpu
from jax.sharding import PartitionSpec as P

epsilon = 1e-06
MESH = pl.DeviceIdType.MESH
BF16 = jnp.bfloat16
F32 = jnp.float32

N = 32
TOK = 128
D = 2048
FF = 704
MAIN = 8
REST = 2
QUAD = 256
RELAY = 31
LAG = 2
CHUNKS = 5


OFFSETS = sorted(((i, j) for i in range(4) for j in range(4)), key=lambda o: -min(o[0], 4 - o[0]) - min(o[1], 4 - o[1]))


def plane_peers(e):
    x, y, core = e // 8, (e // 2) % 4, e % 2
    columns = [((x + i) % 4) * 8 for i in range(4)]
    lines = [((y + j) % 4) * 2 for j in range(4)]
    for i, j in OFFSETS:
        if (i, j) != (0, 0):
            yield columns[i] + lines[j] + core
        yield columns[i] + lines[j] + 1 - core


def drain(ref, count, sem):
    pltpu.make_async_copy(ref.at[pl.ds(0, count)], ref.at[pl.ds(0, count)], sem).wait()


def iota(shape, dim):
    return lax.broadcasted_iota(jnp.int32, shape, dim)


def onehot(cond):
    return jnp.where(cond, 1.0, 0.0).astype(BF16)


def slots_of(routes):
    own = [jnp.where(iota((N, TOK), 0) == routes[k : k + 1], 1.0, 0.0) for k in range(2)]
    before = jnp.where(iota((TOK, TOK), 0) < iota((TOK, TOK), 1), 1.0, 0.0).astype(BF16)
    earlier = [jnp.dot(o.astype(BF16), before, preferred_element_type=F32) for o in own]
    first = jnp.sum(own[0], axis=1, keepdims=True)
    rank0 = jnp.sum(own[0] * earlier[0], axis=0, keepdims=True)
    rank1 = jnp.sum(own[1] * (earlier[1] + first), axis=0, keepdims=True)
    return [rank0.astype(jnp.int32), rank1.astype(jnp.int32)]


def kernel(
    tok_hbm, routes_hbm, codes_hbm, table_ref, wg_hbm, wu_hbm, wd_hbm, gain_hbm, out_ref,
    tok, routes, codes, gain, wg, wu, wd,
    send, recv, rest_x, gate, up, hid, mix, fold, unfold, ret_s, ret_r, back_x, z_s, z_r, inv_s, inv_r, ssq,
    load_sem, send_sem, recv_sem, rsend_sem, rrecv_sem, zsend_sem, zrecv_sem, isend_sem, irecv_sem, plane_sem, open_sem,
):
    z = lax.axis_index("dp")
    e = lax.axis_index("expert")

    bar = pltpu.get_barrier_semaphore()

    @pl.loop(1, N)
    def _(d):
        @pl.when(e ^ d != RELAY)
        def _():
            pl.semaphore_signal(bar, 1, device_id={"expert": e ^ d}, device_id_type=MESH)

    loads = [
        pltpu.make_async_copy(a, b, load_sem.at[i])
        for i, (a, b) in enumerate(
            [(tok_hbm, tok), (routes_hbm, routes), (codes_hbm, codes), (gain_hbm, gain), (wg_hbm, wg), (wu_hbm, wu), (wd_hbm, wd)]
        )
    ]
    for load in loads:
        load.start()
    for load in loads[:3]:
        load.wait()

    to = [routes[k : k + 1, :] for k in range(2)]
    rank = slots_of(routes[...])
    main_at = [jnp.where(r < MAIN, t * MAIN + r, -1) for t, r in zip(to, rank)]
    rest_at = [jnp.where(r >= MAIN, t * REST + r - MAIN, -1) for t, r in zip(to, rank)]

    rows = iota((N * MAIN, TOK), 0)
    pick = onehot((rows == main_at[0]) | (rows == main_at[1]))
    for c in range(4):
        both = jnp.dot(pick, tok[:, c * 512 : (c + 1) * 512], preferred_element_type=F32)
        folded = jnp.stack([both[:, :256].reshape(N, 8, 256), both[:, 256:].reshape(N, 8, 256)], axis=1)
        send[c * N : (c + 1) * N] = folded.reshape(N, 16, 256).astype(BF16)
    rows = iota((N * 16, TOK), 0)
    held = (rows // 8 == rest_at[0]) | (rows // 8 == rest_at[1])
    total = jnp.zeros((N * 16, 256), F32)
    for q in range(8):
        part = onehot(held & (rows % 8 == q))
        total += jnp.dot(part, tok[:, q * 256 : (q + 1) * 256], preferred_element_type=F32)
    send[4 * N : 5 * N] = total.reshape(N, 16, 256).astype(BF16)

    at = iota((N * 16, N * 16), 0)
    unfold[...] = onehot(iota((N * 16, N * 16), 1) == (at % 64) * 8 + at // 64)
    fold[...] = onehot(iota((N * 16, N * 16), 1) == (at % 8) * 64 + at // 8)

    @pl.when(e != RELAY)
    def _():
        pl.semaphore_wait(bar, N - 1)

    @pl.when(e == RELAY - 1)
    def _():
        pl.semaphore_signal(plane_sem, 1, device_id={"expert": RELAY}, device_id_type=MESH)

    @pl.when(e == RELAY)
    def _():
        pl.semaphore_wait(plane_sem, 1)

        @pl.loop(1, N)
        def _(d):
            pl.semaphore_signal(bar, 1, device_id={"dp": (z + d) % N}, device_id_type=MESH)

    peers = list(plane_peers(e))

    @pl.loop(0, CHUNKS)
    def _(i):
        c = (i + 4) % CHUNKS
        for t in peers:
            pltpu.make_async_remote_copy(
                send.at[c * N + t], recv.at[c * N + e], send_sem, recv_sem.at[c], device_id={"expert": t}, device_id_type=MESH
            ).start()
        recv[c * N + e] = send[c * N + e]

    weight = [jnp.zeros((1, TOK), F32) for _ in range(2)]
    for k in range(2):
        for level in range(16):
            weight[k] = jnp.where(codes[k : k + 1, :] == level, table_ref[level], weight[k])
    rows = iota((384, TOK), 0)
    wide = jnp.zeros((384, TOK), F32)
    for k in range(2):
        wide += jnp.where(rows == jnp.where(rank[k] < MAIN, main_at[k], N * MAIN + rest_at[k]), weight[k], 0.0)
    wide = wide.T[:, :320]
    high = wide.astype(BF16)
    mix[:TOK] = high
    mix[TOK:] = (wide - high.astype(F32)).astype(BF16)
    ssq[...] = jnp.zeros_like(ssq)

    for load in loads[4:6]:
        load.wait()
    drain(recv, N - 1, recv_sem.at[4])
    rest_x[...] = jnp.dot(unfold[...], recv[4 * N : 5 * N].reshape(N * 16, 256), preferred_element_type=F32).astype(BF16)
    for c in range(4):
        drain(recv, N - 1, recv_sem.at[c])
        halves = [
            jnp.concatenate(
                [recv[c * N : (c + 1) * N, h * 8 : (h + 1) * 8].reshape(N * 8, 256), rest_x[(2 * c + h) * 64 : (2 * c + h + 1) * 64]],
                axis=0,
            )
            for h in range(2)
        ]
        x = jnp.concatenate(halves, axis=1)
        for w, acc in ((wg, gate), (wu, up)):
            part = lax.dot_general(x, w[:, c * 512 : (c + 1) * 512], (((1,), (1,)), ((), ())), preferred_element_type=F32)
            if c == 0:
                acc[...] = part
            else:
                acc[...] += part
    g = gate[...]
    hid[...] = (g / (1.0 + jnp.exp(-g)) * up[...]).astype(BF16)
    loads[6].wait()
    loads[3].wait()

    def quad_of(k):
        far = (k + 1) // 2
        return (z // 4 + 4 + jnp.where(k % 2 == 1, -far, far)) % 8

    def columns(quad):
        return wd[:, pl.ds(pl.multiple_of(quad * QUAD, QUAD), QUAD)]

    def give_back(at, block):
        ret_s[pl.ds(at * N, N)] = block.reshape(N, 16, 128).astype(BF16)

        for t in peers:
            pltpu.make_async_remote_copy(
                ret_s.at[at * N + t], ret_r.at[at * N + e], rsend_sem, rrecv_sem.at[at], device_id={"expert": t}, device_id_type=MESH
            ).start()

        ret_r[at * N + e] = ret_s[at * N + e]

    def expert_rest(half):
        pieces = []
        for i in range(4):
            out = jnp.dot(hid[N * MAIN :], columns(quad_of(half * 4 + i)), preferred_element_type=F32).astype(BF16)
            pieces += [out[:, :128], out[:, 128:]]
        give_back(8 + half, jnp.dot(fold[...], jnp.concatenate(pieces, axis=0), preferred_element_type=F32))

    def expert_main(k):
        out = jnp.dot(hid[: N * MAIN], columns(quad_of(k)), preferred_element_type=F32)
        give_back(k, jnp.stack([out[:, :128].reshape(N, 8, 128), out[:, 128:].reshape(N, 8, 128)], axis=1))

    def home_rest(half):
        drain(ret_r, N - 1, rrecv_sem.at[8 + half])
        block = ret_r[pl.ds((8 + half) * N, N)].reshape(N * 16, 128)
        back_x[...] = jnp.dot(unfold[...], block, preferred_element_type=F32).reshape(8, 64, 128).astype(BF16)

    def home_main(k):
        quad = quad_of(k)
        drain(ret_r, N - 1, rrecv_sem.at[k])
        halves = [
            jnp.concatenate([ret_r[pl.ds(k * N, N), h * 8 : (h + 1) * 8].reshape(N * 8, 128), back_x[2 * (k % 4) + h]], axis=0)
            for h in range(2)
        ]
        block = jnp.concatenate(halves, axis=1)
        pair = jnp.dot(mix[...], block, preferred_element_type=F32)
        comb = (pair[:TOK] + pair[TOK:]).astype(BF16).astype(F32).T
        ssq[...] += jnp.sum(comb * comb, axis=0, keepdims=True)
        base = pl.multiple_of(quad * QUAD, QUAD)
        z_s[pl.ds(base, QUAD)] = comb.astype(BF16)

        @pl.loop(0, 4)
        def _(b):
            t = quad * 4 + b

            @pl.when(t != z)
            def _():
                pltpu.make_async_remote_copy(
                    z_s.at[pl.ds(pl.multiple_of(t * 64, 64), 64)], z_r.at[z], zsend_sem, zrecv_sem, device_id={"dp": t}, device_id_type=MESH
                ).start()

    @pl.loop(0, 8 + LAG)
    def _(k):
        @pl.when((k == 0) | (k == 4))
        def _():
            expert_rest(k // 4)

        @pl.when(k < 8)
        def _():
            expert_main(k)

        @pl.when((k == LAG) & (e == RELAY))
        def _():
            pl.semaphore_wait(bar, N - 1)

            @pl.loop(1, N)
            def _(d):
                pl.semaphore_signal(open_sem, 1, device_id={"expert": e ^ d}, device_id_type=MESH)

        @pl.when((k == LAG) & (e != RELAY))
        def _():
            pl.semaphore_wait(open_sem, 1)

        @pl.when((k == LAG) | (k == LAG + 4))
        def _():
            home_rest((k - LAG) // 4)

        @pl.when(k >= LAG)
        def _():
            home_main(k - LAG)

    inv_s[...] = lax.rsqrt(ssq[...] * (1.0 / D) + epsilon)

    @pl.loop(1, N)
    def _(d):
        pltpu.make_async_remote_copy(
            inv_s, inv_r.at[z], isend_sem, irecv_sem, device_id={"dp": (z + d) % N}, device_id_type=MESH
        ).start()

    inv_r[z] = inv_s[...]
    z_r[z] = z_s[pl.ds(pl.multiple_of(z * 64, 64), 64)]

    line = jnp.broadcast_to(gain[pl.ds(z // 2, 1), :], (64, 128))
    mine = iota((64, 128), 1) == iota((64, 128), 0) + 64 * (z % 2)
    column = jnp.sum(jnp.where(mine, line, 0.0), axis=1, keepdims=True)

    drain(send, CHUNKS * (N - 1), send_sem)
    drain(ret_s, 10 * (N - 1), rsend_sem)
    drain(z_s, (N - 1) * 64, zsend_sem)
    drain(inv_r, N - 1, isend_sem)
    drain(z_r, N - 1, zrecv_sem)
    drain(inv_r, N - 1, irecv_sem)
    for s in range(N):
        out_ref[:, s * TOK : (s + 1) * TOK] = (z_r[s].astype(F32) * inv_r[s] * column).astype(BF16)


def local(tokens, routes, gate_code, gate_table, w_gate, w_up, w_down, norm_gain):
    anywhere = pl.BlockSpec(memory_space=pl.ANY)
    dma = pltpu.SemaphoreType.DMA
    relaid = pl.pallas_call(
        kernel,
        out_shape=jax.ShapeDtypeStruct((D // N, N * TOK), BF16),
        in_specs=[anywhere] * 3 + [pl.BlockSpec(memory_space=pltpu.SMEM)] + [anywhere] * 4,
        out_specs=pl.BlockSpec(memory_space=pltpu.VMEM),
        scratch_shapes=[
            pltpu.VMEM((TOK, D), BF16),
            pltpu.VMEM((2, TOK), jnp.int32),
            pltpu.VMEM((2, TOK), jnp.int32),
            pltpu.VMEM((16, 128), F32),
            pltpu.VMEM((FF, D), BF16),
            pltpu.VMEM((FF, D), BF16),
            pltpu.VMEM((FF, D), BF16),
            pltpu.VMEM((CHUNKS * N, 16, 256), BF16),
            pltpu.VMEM((CHUNKS * N, 16, 256), BF16),
            pltpu.VMEM((N * 16, 256), BF16),
            pltpu.VMEM((320, FF), F32),
            pltpu.VMEM((320, FF), F32),
            pltpu.VMEM((320, FF), BF16),
            pltpu.VMEM((2 * TOK, 320), BF16),
            pltpu.VMEM((N * 16, N * 16), BF16),
            pltpu.VMEM((N * 16, N * 16), BF16),
            pltpu.VMEM((10 * N, 16, 128), BF16),
            pltpu.VMEM((10 * N, 16, 128), BF16),
            pltpu.VMEM((8, 64, 128), BF16),
            pltpu.VMEM((D, TOK), BF16),
            pltpu.VMEM((N, 64, TOK), BF16),
            pltpu.VMEM((1, TOK), F32),
            pltpu.VMEM((N, 1, TOK), F32),
            pltpu.VMEM((1, TOK), F32),
            dma((7,)), dma, dma((CHUNKS,)), dma, dma((10,)), dma, dma, dma, dma,
            pltpu.SemaphoreType.REGULAR, pltpu.SemaphoreType.REGULAR,
        ],
        compiler_params=pltpu.CompilerParams(collective_id=0, has_side_effects=True, vmem_limit_bytes=63 << 20),
        cost_estimate=pl.CostEstimate(flops=3 << 30, bytes_accessed=10 << 20, transcendentals=320 * FF),
    )(
        tokens[0],
        routes[0].T,
        gate_code[0].T,
        gate_table,
        jnp.swapaxes(w_gate[0], 0, 1),
        jnp.swapaxes(w_up[0], 0, 1),
        w_down[0],
        norm_gain.reshape(16, 128),
    )
    return relaid.T[None]


def solution(mesh):
    in_specs = (
        P("expert", "dp", None),
        P("expert", "dp", None),
        P("expert", "dp", None),
        P(),
        P("expert", None, None),
        P("expert", None, None),
        P("expert", None, None),
        P(),
    )
    out_specs = P("expert", None, "dp")
    return jax.shard_map(local, mesh=mesh, in_specs=in_specs, out_specs=out_specs, check_vma=False)
```

```python
import functools

import jax
import jax.numpy as jnp
from jax import lax
from jax.experimental import pallas as pl
from jax.experimental.pallas import tpu as pltpu
from jax.sharding import PartitionSpec as P

epsilon = 1e-06
MESH = pl.DeviceIdType.MESH
BF16 = jnp.bfloat16
F32 = jnp.float32

N = 32
TOK = 128
D = 2048
FF = 704
MAIN = 8
REST = 2
QUAD = 256
RELAY = 31
LAG = 2
CHUNKS = 5


OFFSETS = sorted(((i, j) for i in range(4) for j in range(4)), key=lambda o: -min(o[0], 4 - o[0]) - min(o[1], 4 - o[1]))


def plane_peers(e):
    x, y, core = e // 8, (e // 2) % 4, e % 2
    columns = [((x + i) % 4) * 8 for i in range(4)]
    lines = [((y + j) % 4) * 2 for j in range(4)]
    for i, j in OFFSETS:
        if (i, j) != (0, 0):
            yield columns[i] + lines[j] + core
        yield columns[i] + lines[j] + 1 - core


def drain(ref, count, sem):
    pltpu.make_async_copy(ref.at[pl.ds(0, count)], ref.at[pl.ds(0, count)], sem).wait()


def iota(shape, dim):
    return lax.broadcasted_iota(jnp.int32, shape, dim)


def onehot(cond):
    return jnp.where(cond, 1.0, 0.0).astype(BF16)


def slots_of(routes):
    own = [jnp.where(iota((N, TOK), 0) == routes[k : k + 1], 1.0, 0.0) for k in range(2)]
    before = jnp.where(iota((TOK, TOK), 0) < iota((TOK, TOK), 1), 1.0, 0.0).astype(BF16)
    earlier = [jnp.dot(o.astype(BF16), before, preferred_element_type=F32) for o in own]
    first = jnp.sum(own[0], axis=1, keepdims=True)
    rank0 = jnp.sum(own[0] * earlier[0], axis=0, keepdims=True)
    rank1 = jnp.sum(own[1] * (earlier[1] + first), axis=0, keepdims=True)
    return [rank0.astype(jnp.int32), rank1.astype(jnp.int32)]


def kernel(
    tok_hbm, routes_hbm, codes_hbm, table_ref, wg_hbm, wu_hbm, wd_hbm, gain_hbm, out_ref,
    tok, routes, codes, gain, wg, wu, wd,
    send, recv, rest_x, gate, up, hid, mix, fold, unfold, ret_s, ret_r, back_x, z_s, z_r, inv_s, inv_r, ssq,
    load_sem, send_sem, recv_sem, rsend_sem, rrecv_sem, zsend_sem, zrecv_sem, isend_sem, irecv_sem, plane_sem, open_sem,
):
    z = lax.axis_index("dp")
    e = lax.axis_index("expert")

    bar = pltpu.get_barrier_semaphore()

    @pl.loop(1, N)
    def _(d):
        @pl.when(e ^ d != RELAY)
        def _():
            pl.semaphore_signal(bar, 1, device_id={"expert": e ^ d}, device_id_type=MESH)

    loads = [
        pltpu.make_async_copy(a, b, load_sem.at[i])
        for i, (a, b) in enumerate(
            [(tok_hbm, tok), (routes_hbm, routes), (codes_hbm, codes), (gain_hbm, gain), (wg_hbm, wg), (wu_hbm, wu), (wd_hbm, wd)]
        )
    ]
    for load in loads:
        load.start()
    for load in loads[:3]:
        load.wait()

    to = [routes[k : k + 1, :] for k in range(2)]
    rank = slots_of(routes[...])
    main_at = [jnp.where(r < MAIN, t * MAIN + r, -1) for t, r in zip(to, rank)]
    rest_at = [jnp.where(r >= MAIN, t * REST + r - MAIN, -1) for t, r in zip(to, rank)]

    rows = iota((N * MAIN, TOK), 0)
    pick = onehot((rows == main_at[0]) | (rows == main_at[1]))
    for c in range(4):
        both = jnp.dot(pick, tok[:, c * 512 : (c + 1) * 512], preferred_element_type=F32)
        folded = jnp.stack([both[:, :256].reshape(N, 8, 256), both[:, 256:].reshape(N, 8, 256)], axis=1)
        send[c * N : (c + 1) * N] = folded.reshape(N, 16, 256).astype(BF16)
    rows = iota((N * 16, TOK), 0)
    held = (rows // 8 == rest_at[0]) | (rows // 8 == rest_at[1])
    total = jnp.zeros((N * 16, 256), F32)
    for q in range(8):
        part = onehot(held & (rows % 8 == q))
        total += jnp.dot(part, tok[:, q * 256 : (q + 1) * 256], preferred_element_type=F32)
    send[4 * N : 5 * N] = total.reshape(N, 16, 256).astype(BF16)

    at = iota((N * 16, N * 16), 0)
    unfold[...] = onehot(iota((N * 16, N * 16), 1) == (at % 64) * 8 + at // 64)
    fold[...] = onehot(iota((N * 16, N * 16), 1) == (at % 8) * 64 + at // 8)

    @pl.when(e != RELAY)
    def _():
        pl.semaphore_wait(bar, N - 1)

    @pl.when(e == RELAY - 1)
    def _():
        pl.semaphore_signal(plane_sem, 1, device_id={"expert": RELAY}, device_id_type=MESH)

    @pl.when(e == RELAY)
    def _():
        pl.semaphore_wait(plane_sem, 1)

        @pl.loop(1, N)
        def _(d):
            pl.semaphore_signal(bar, 1, device_id={"dp": (z + d) % N}, device_id_type=MESH)

    peers = list(plane_peers(e))

    @pl.loop(0, CHUNKS)
    def _(i):
        c = (i + 4) % CHUNKS
        for t in peers:
            pltpu.make_async_remote_copy(
                send.at[c * N + t], recv.at[c * N + e], send_sem, recv_sem.at[c], device_id={"expert": t}, device_id_type=MESH
            ).start()
        recv[c * N + e] = send[c * N + e]

    weight = [jnp.zeros((1, TOK), F32) for _ in range(2)]
    for k in range(2):
        for level in range(16):
            weight[k] = jnp.where(codes[k : k + 1, :] == level, table_ref[level], weight[k])
    rows = iota((384, TOK), 0)
    wide = jnp.zeros((384, TOK), F32)
    for k in range(2):
        wide += jnp.where(rows == jnp.where(rank[k] < MAIN, main_at[k], N * MAIN + rest_at[k]), weight[k], 0.0)
    wide = wide.T[:, :320]
    high = wide.astype(BF16)
    mix[:TOK] = high
    mix[TOK:] = (wide - high.astype(F32)).astype(BF16)
    ssq[...] = jnp.zeros_like(ssq)

    for load in loads[4:6]:
        load.wait()
    drain(recv, N - 1, recv_sem.at[4])
    rest_x[...] = jnp.dot(unfold[...], recv[4 * N : 5 * N].reshape(N * 16, 256), preferred_element_type=F32).astype(BF16)
    for c in range(4):
        drain(recv, N - 1, recv_sem.at[c])
        halves = [
            jnp.concatenate(
                [recv[c * N : (c + 1) * N, h * 8 : (h + 1) * 8].reshape(N * 8, 256), rest_x[(2 * c + h) * 64 : (2 * c + h + 1) * 64]],
                axis=0,
            )
            for h in range(2)
        ]
        x = jnp.concatenate(halves, axis=1)
        for w, acc in ((wg, gate), (wu, up)):
            part = lax.dot_general(x, w[:, c * 512 : (c + 1) * 512], (((1,), (1,)), ((), ())), preferred_element_type=F32)
            if c == 0:
                acc[...] = part
            else:
                acc[...] += part
    g = gate[...]
    hid[...] = (g / (1.0 + jnp.exp(-g)) * up[...]).astype(BF16)
    loads[6].wait()
    loads[3].wait()

    def quad_of(k):
        far = (k + 1) // 2
        return (z // 4 + 4 + jnp.where(k % 2 == 1, -far, far)) % 8

    def columns(quad):
        return wd[:, pl.ds(pl.multiple_of(quad * QUAD, QUAD), QUAD)]

    def give_back(at, block):
        ret_s[pl.ds(at * N, N)] = block.reshape(N, 16, 128).astype(BF16)

        for t in peers:
            pltpu.make_async_remote_copy(
                ret_s.at[at * N + t], ret_r.at[at * N + e], rsend_sem, rrecv_sem.at[at], device_id={"expert": t}, device_id_type=MESH
            ).start()

        ret_r[at * N + e] = ret_s[at * N + e]

    def expert_rest(half):
        pieces = []
        for i in range(4):
            out = jnp.dot(hid[N * MAIN :], columns(quad_of(half * 4 + i)), preferred_element_type=F32).astype(BF16)
            pieces += [out[:, :128], out[:, 128:]]
        give_back(8 + half, jnp.dot(fold[...], jnp.concatenate(pieces, axis=0), preferred_element_type=F32))

    def expert_main(k):
        out = jnp.dot(hid[: N * MAIN], columns(quad_of(k)), preferred_element_type=F32)
        give_back(k, jnp.stack([out[:, :128].reshape(N, 8, 128), out[:, 128:].reshape(N, 8, 128)], axis=1))

    def home_rest(half):
        drain(ret_r, N - 1, rrecv_sem.at[8 + half])
        block = ret_r[pl.ds((8 + half) * N, N)].reshape(N * 16, 128)
        back_x[...] = jnp.dot(unfold[...], block, preferred_element_type=F32).reshape(8, 64, 128).astype(BF16)

    def home_main(k):
        quad = quad_of(k)
        drain(ret_r, N - 1, rrecv_sem.at[k])
        halves = [
            jnp.concatenate([ret_r[pl.ds(k * N, N), h * 8 : (h + 1) * 8].reshape(N * 8, 128), back_x[2 * (k % 4) + h]], axis=0)
            for h in range(2)
        ]
        block = jnp.concatenate(halves, axis=1)
        pair = jnp.dot(mix[...], block, preferred_element_type=F32)
        comb = (pair[:TOK] + pair[TOK:]).astype(BF16).astype(F32).T
        ssq[...] += jnp.sum(comb * comb, axis=0, keepdims=True)
        base = pl.multiple_of(quad * QUAD, QUAD)
        z_s[pl.ds(base, QUAD)] = comb.astype(BF16)

        @pl.loop(0, 4)
        def _(b):
            t = quad * 4 + b

            @pl.when(t != z)
            def _():
                pltpu.make_async_remote_copy(
                    z_s.at[pl.ds(pl.multiple_of(t * 64, 64), 64)], z_r.at[z], zsend_sem, zrecv_sem, device_id={"dp": t}, device_id_type=MESH
                ).start()

    @pl.loop(0, 8 + LAG)
    def _(k):
        @pl.when(k < 8)
        def _():
            expert_main(k)

        @pl.when((k == 0) | (k == 4))
        def _():
            expert_rest(k // 4)

        @pl.when((k == LAG) & (e == RELAY))
        def _():
            pl.semaphore_wait(bar, N - 1)

            @pl.loop(1, N)
            def _(d):
                pl.semaphore_signal(open_sem, 1, device_id={"expert": e ^ d}, device_id_type=MESH)

        @pl.when((k == LAG) & (e != RELAY))
        def _():
            pl.semaphore_wait(open_sem, 1)

        @pl.when((k == LAG) | (k == LAG + 4))
        def _():
            home_rest((k - LAG) // 4)

        @pl.when(k >= LAG)
        def _():
            home_main(k - LAG)

    inv_s[...] = lax.rsqrt(ssq[...] * (1.0 / D) + epsilon)

    @pl.loop(1, N)
    def _(d):
        pltpu.make_async_remote_copy(
            inv_s, inv_r.at[z], isend_sem, irecv_sem, device_id={"dp": (z + d) % N}, device_id_type=MESH
        ).start()

    inv_r[z] = inv_s[...]
    z_r[z] = z_s[pl.ds(pl.multiple_of(z * 64, 64), 64)]

    line = jnp.broadcast_to(gain[pl.ds(z // 2, 1), :], (64, 128))
    mine = iota((64, 128), 1) == iota((64, 128), 0) + 64 * (z % 2)
    column = jnp.sum(jnp.where(mine, line, 0.0), axis=1, keepdims=True)

    drain(send, CHUNKS * (N - 1), send_sem)
    drain(ret_s, 10 * (N - 1), rsend_sem)
    drain(z_s, (N - 1) * 64, zsend_sem)
    drain(inv_r, N - 1, isend_sem)
    drain(z_r, N - 1, zrecv_sem)
    drain(inv_r, N - 1, irecv_sem)
    for s in range(N):
        out_ref[:, s * TOK : (s + 1) * TOK] = (z_r[s].astype(F32) * inv_r[s] * column).astype(BF16)


def local(tokens, routes, gate_code, gate_table, w_gate, w_up, w_down, norm_gain):
    anywhere = pl.BlockSpec(memory_space=pl.ANY)
    dma = pltpu.SemaphoreType.DMA
    relaid = pl.pallas_call(
        kernel,
        out_shape=jax.ShapeDtypeStruct((D // N, N * TOK), BF16),
        in_specs=[anywhere] * 3 + [pl.BlockSpec(memory_space=pltpu.SMEM)] + [anywhere] * 4,
        out_specs=pl.BlockSpec(memory_space=pltpu.VMEM),
        scratch_shapes=[
            pltpu.VMEM((TOK, D), BF16),
            pltpu.VMEM((2, TOK), jnp.int32),
            pltpu.VMEM((2, TOK), jnp.int32),
            pltpu.VMEM((16, 128), F32),
            pltpu.VMEM((FF, D), BF16),
            pltpu.VMEM((FF, D), BF16),
            pltpu.VMEM((FF, D), BF16),
            pltpu.VMEM((CHUNKS * N, 16, 256), BF16),
            pltpu.VMEM((CHUNKS * N, 16, 256), BF16),
            pltpu.VMEM((N * 16, 256), BF16),
            pltpu.VMEM((320, FF), F32),
            pltpu.VMEM((320, FF), F32),
            pltpu.VMEM((320, FF), BF16),
            pltpu.VMEM((2 * TOK, 320), BF16),
            pltpu.VMEM((N * 16, N * 16), BF16),
            pltpu.VMEM((N * 16, N * 16), BF16),
            pltpu.VMEM((10 * N, 16, 128), BF16),
            pltpu.VMEM((10 * N, 16, 128), BF16),
            pltpu.VMEM((8, 64, 128), BF16),
            pltpu.VMEM((D, TOK), BF16),
            pltpu.VMEM((N, 64, TOK), BF16),
            pltpu.VMEM((1, TOK), F32),
            pltpu.VMEM((N, 1, TOK), F32),
            pltpu.VMEM((1, TOK), F32),
            dma((7,)), dma, dma((CHUNKS,)), dma, dma((10,)), dma, dma, dma, dma,
            pltpu.SemaphoreType.REGULAR, pltpu.SemaphoreType.REGULAR,
        ],
        compiler_params=pltpu.CompilerParams(collective_id=0, has_side_effects=True, vmem_limit_bytes=63 << 20),
        cost_estimate=pl.CostEstimate(flops=3 << 30, bytes_accessed=10 << 20, transcendentals=320 * FF),
    )(
        tokens[0],
        routes[0].T,
        gate_code[0].T,
        gate_table,
        jnp.swapaxes(w_gate[0], 0, 1),
        jnp.swapaxes(w_up[0], 0, 1),
        w_down[0],
        norm_gain.reshape(16, 128),
    )
    return relaid.T[None]


def solution(mesh):
    in_specs = (
        P("expert", "dp", None),
        P("expert", "dp", None),
        P("expert", "dp", None),
        P(),
        P("expert", None, None),
        P("expert", None, None),
        P("expert", None, None),
        P(),
    )
    out_specs = P("expert", None, "dp")
    return jax.shard_map(local, mesh=mesh, in_specs=in_specs, out_specs=out_specs, check_vma=False)
```
